256 devices in a mesh: seq: 64 (over x, z, core), head: 4 (over y).
Axes of the slice: x: 4, y: 4, z: 8, core: 2. Of those that a mesh axis runs over, the one named last changes fastest.
Arguments:
- queries: bfloat16 [256, 8192], P('seq', 'head'), may hold values from -150 to 150
- prompt_keys: bfloat16 [131072, 1024], P('seq', 'head'), may hold values from -4 to 4
- prompt_values: bfloat16 [131072, 1024], P('seq', 'head'), may hold values from -6 to 6
- generated_keys: bfloat16 [256, 2048, 1024], P('seq', None, 'head'), may hold values from -8 to 8
- generated_values: bfloat16 [256, 2048, 1024], P('seq', None, 'head'), may hold values from -6 to 6
- suffix_lengths: int32 [256], P('seq'), may hold values from 1 to 2048, 262144 in all
- slot_sample: int32 [256], P('seq'), may hold values from 0 to 255, each once
- out_weight: bfloat16 [8192, 8192], P('head', 'seq'), may hold values from -0.0625 to 0.0625
Outputs:
- mixed: bfloat16 [256, 8192], P('head', 'seq')
The draws below stay inside these ranges and needn't reach their ends.
Inputs may be any that keep to these rules, and one draw needn't show every extreme that they name: `suffix_lengths`: some slot's length equals 2048. `slot_sample`: each sample id appears in exactly one slot.
All inputs are finite; a program needn't handle non-finite values. No bound on the sum of `suffix_lengths` on one device may be relied on, other than what follows from the above.
Results may differ from the reference program's by a relative error of at most 0.015.
Values may be sent and summed in bfloat16 or wider, within the bound.
No kernel may reach another device: no remote copies, remote signals or barrier semaphores. Data moves between devices by JAX's collectives and lax.ppermute only.
A program may use at most 128 MiB of HBM per device.

```python
import math
import jax
import jax.numpy as jnp
import numpy as np
from jax import lax

D = 8192
QUERY_HEADS = 64
KEY_VALUE_HEADS = 8
HEAD_WIDTH = 128
SUFFIX_CAPACITY = 2048
PROMPT_LENGTH = 131072
SAMPLE_TOTAL = 256


def shared_keys(key, twin):
    model_width = KEY_VALUE_HEADS * HEAD_WIDTH
    pairs = PROMPT_LENGTH // 2
    base = jnp.clip(jax.random.normal(jax.random.fold_in(key, 101), (PROMPT_LENGTH, model_width), jnp.float32), -4.0, 4.0)
    offset = jax.random.randint(jax.random.fold_in(key, 103), (), 0, 8)
    paired = base.reshape(pairs, 2, model_width)
    strength = min(twin * 1000.0, 1.0)
    chosen = (jnp.arange(pairs) % 8 == offset).astype(jnp.float32)[:, None] * strength
    second = paired[:, 1] * (1.0 - chosen)
    key_output = jnp.stack([paired[:, 0], second], axis=1).reshape(PROMPT_LENGTH, model_width)
    return key_output


def draw_prompt_keys(key, part):
    key_output = shared_keys(key, 0.0)
    return key_output.astype(jnp.bfloat16)


def draw_queries(key, part):
    key = jax.random.fold_in(key, 5)
    result = 3.0 * jax.random.normal(jax.random.fold_in(key, 1), (SAMPLE_TOTAL, QUERY_HEADS * HEAD_WIDTH), jnp.float32)
    return jnp.clip(result, -15.0, 15.0).astype(jnp.bfloat16)


def block_scale(rng, dims, pieces, low, high):
    def one(axis_at, shards_of):
        heights = jax.random.uniform(jax.random.fold_in(jax.random.fold_in(rng, 6), axis_at), (shards_of,), jnp.float32, low / len(pieces), high / len(pieces))
        return jnp.repeat(jnp.exp(heights), dims[axis_at] // shards_of).reshape((-1,) + (1,) * (len(dims) - axis_at - 1))

    gain = one(*pieces[0])
    for cut in pieces[1:]:
        gain = gain * one(*cut)
    return gain


def profile(count, total, most, slope):
    weights = [(1 << 20) // math.isqrt(standing ** slope) + 1 for standing in range(2, count + 1)]
    surplus, counts = total - most - (count - 1), [1] * (count - 1)
    while surplus > 0:
        free = [i for i in range(count - 1) if counts[i] < most]
        pool, left = sum([weights[i] for i in free]), surplus
        for i in free:
            addition = min(most - counts[i], max(1, left * weights[i] // pool), surplus)
            counts[i] = counts[i] + addition
            surplus = surplus - addition
    return np.array([most] + counts)


def uneven(stream_key, number_of, total, reach, skew):
    if number_of == 2:
        one = jax.random.randint(stream_key, (), max(1, total - reach), min(reach, total - 1) + 1)
        return jnp.stack([one, total - one])
    tallies = jnp.asarray(profile(number_of, total, reach, skew), jnp.int32)
    twos = (number_of - 1) // 2
    source_of, sink = tallies[1:1 + 2 * twos:2], tallies[2:2 + 2 * twos:2]
    slack = jnp.minimum(source_of - 1, reach - sink)
    shifted = jax.random.randint(jax.random.fold_in(stream_key, 1), (twos,), 0, 1 << 20) % (slack + 1)
    tallies = tallies.at[1:1 + 2 * twos:2].set(source_of - shifted).at[2:2 + 2 * twos:2].set(sink + shifted)
    return tallies[jax.random.permutation(jax.random.fold_in(stream_key, 2), number_of)]


def normal_values(stream_key, dims, scale, limit, split=(), dtype=jnp.bfloat16):
    drawn = jax.random.normal(stream_key, dims, jnp.float32) * scale
    if len(split) > 0:
        drawn = block_scale(stream_key, dims, split, -0.22, 0.18) * drawn
    return jnp.clip(drawn, min=-limit, max=limit).astype(dtype)


def setup_inputs(seed: int = 0) -> dict:
    arg_keys = jax.random.split(jax.random.key(seed), 9)
    return {
        "queries": draw_queries(jax.random.fold_in(arg_keys[8], 71), 0),
        "prompt_keys": draw_prompt_keys(jax.random.fold_in(arg_keys[8], 71), 0),
        "prompt_values": normal_values(arg_keys[2], (PROMPT_LENGTH, KEY_VALUE_HEADS * HEAD_WIDTH), 1.0, 6.0, ((0, 64), (1, 4))),
        "generated_keys": normal_values(arg_keys[3], (SAMPLE_TOTAL, SUFFIX_CAPACITY, KEY_VALUE_HEADS * HEAD_WIDTH), 1.4, 8.0, ((0, 64), (2, 4))),
        "generated_values": normal_values(arg_keys[4], (SAMPLE_TOTAL, SUFFIX_CAPACITY, KEY_VALUE_HEADS * HEAD_WIDTH), 1.0, 6.0, ((0, 64), (2, 4))),
        "suffix_lengths": uneven(arg_keys[5], SAMPLE_TOTAL, SAMPLE_TOTAL * SUFFIX_CAPACITY // 2, SUFFIX_CAPACITY, 2).astype(jnp.int32),
        "slot_sample": jax.random.permutation(arg_keys[6], SAMPLE_TOTAL).astype(jnp.int32),
        "out_weight": normal_values(arg_keys[7], (QUERY_HEADS * HEAD_WIDTH, D), (QUERY_HEADS * HEAD_WIDTH) ** -0.5, 0.0625, ((0, 4), (1, 64))),
    }


def reference(queries, prompt_keys, prompt_values, generated_keys, generated_values, suffix_lengths, slot_sample, out_weight):
    heads_per_group = QUERY_HEADS // KEY_VALUE_HEADS
    scaling = HEAD_WIDTH ** -0.5
    expanded_keys = prompt_keys.astype(jnp.float32).reshape(PROMPT_LENGTH, KEY_VALUE_HEADS, HEAD_WIDTH)
    expanded_values = prompt_values.astype(jnp.float32).reshape(PROMPT_LENGTH, KEY_VALUE_HEADS, HEAD_WIDTH)
    positions = jnp.arange(SUFFIX_CAPACITY)

    def one_slot(inputs):
        single_query, sample_keys, sample_values, length = inputs
        query_head_count = single_query.astype(jnp.float32).reshape(KEY_VALUE_HEADS, heads_per_group, HEAD_WIDTH)
        sample_keys = sample_keys.astype(jnp.float32).reshape(SUFFIX_CAPACITY, KEY_VALUE_HEADS, HEAD_WIDTH)
        sample_values = sample_values.astype(jnp.float32).reshape(SUFFIX_CAPACITY, KEY_VALUE_HEADS, HEAD_WIDTH)
        prompt_scores = jnp.einsum('kgd,pkd->kgp', query_head_count, expanded_keys) * scaling
        suffix_scores = jnp.einsum('kgd,tkd->kgt', query_head_count, sample_keys) * scaling
        suffix_scores = jnp.where(positions < length, suffix_scores, -1e30)
        highest = jnp.maximum(prompt_scores.max(-1), suffix_scores.max(-1))
        prompt_weights = jnp.exp(prompt_scores - highest[..., None])
        suffix_weights = jnp.exp(suffix_scores - highest[..., None])
        total = prompt_weights.sum(-1) + suffix_weights.sum(-1)
        prompt_rounded = lax.optimization_barrier(prompt_weights.astype(jnp.bfloat16))
        suffix_rounded = lax.optimization_barrier(suffix_weights.astype(jnp.bfloat16))
        numerator = jnp.einsum('kgp,pkd->kgd', prompt_rounded.astype(jnp.float32), expanded_values)
        numerator = numerator + jnp.einsum('kgt,tkd->kgd', suffix_rounded.astype(jnp.float32), sample_values)
        return (numerator / total[..., None]).astype(jnp.bfloat16).reshape(QUERY_HEADS * HEAD_WIDTH)

    attention = lax.map(one_slot, (queries, generated_keys, generated_values, suffix_lengths))
    projected = jnp.dot(attention, out_weight, preferred_element_type=jnp.float32)
    ordered = jnp.zeros_like(projected).at[slot_sample].set(projected)
    return ordered.astype(jnp.bfloat16)
```

```python
import functools

import jax
import jax.numpy as jnp
import numpy as np
from jax import lax
from jax.experimental import pallas as pl
from jax.experimental.pallas import tpu as pltpu
from jax.sharding import PartitionSpec as P

HEADS = 16
KV = 2
PER = 8
W = 128
SLOTS = 4
X, Z, CORES, Y = 4, 8, 2, 4
CHIPS = X * Z
ROWS = HEADS * SLOTS
PACKED = ROWS + 16
STEP = 8
MIB = 1 << 20
BF, F32 = jnp.bfloat16, jnp.float32
TO_LOG2 = float(np.log2(np.e) * W**-0.5)
NT = (((1,), (1,)), ((), ()))


def params(limit, steps=0):
    semantics = ("arbitrary",) * steps if steps else None
    return pltpu.CompilerParams(vmem_limit_bytes=limit * MIB, dimension_semantics=semantics)


def spread_kernel(q_ref, out_ref):
    q = q_ref[...].astype(F32)
    block = jnp.concatenate([q[:, h * W : (h + 1) * W] for h in range(HEADS)], axis=0).astype(BF)
    for chip in range(CHIPS):
        out_ref[chip] = block


def spread(queries):
    return pl.pallas_call(
        spread_kernel,
        out_shape=jax.ShapeDtypeStruct((CHIPS, ROWS, W), BF),
        compiler_params=params(8),
        name="spread_queries",
    )(queries)


def suffix_kernel(length_ref, q_ref, k_ref, v_ref, out_ref, lse_ref):
    slot = pl.program_id(0)
    length = length_ref[slot]
    span = k_ref.shape[1]
    for g in range(KV):
        q = q_ref[0, g].astype(BF)
        s = lax.dot_general(q, k_ref[0, :, g * W : (g + 1) * W], NT, preferred_element_type=F32)
        s = s * TO_LOG2
        at = lax.broadcasted_iota(jnp.int32, (PER, span), 1)
        s = jnp.where(at < length, s, -1e30)
        top = jnp.max(s, axis=1, keepdims=True)
        p = jnp.exp2(s - top)
        total = jnp.sum(p, axis=1, keepdims=True)
        o = jnp.dot(p.astype(BF), v_ref[0, :, g * W : (g + 1) * W], preferred_element_type=F32)
        out_ref[g, 0] = o / total
        lse_ref[g, 0] = jnp.broadcast_to(top + jnp.log2(total), (PER, W))


def suffix(lengths, q, keys, values):
    span = keys.shape[1]
    shape = jax.ShapeDtypeStruct((KV, SLOTS, PER, W), F32)
    wide = pl.BlockSpec((1, span, KV * W), lambda s, n: (s, 0, 0))
    out = pl.BlockSpec((KV, 1, PER, W), lambda s, n: (0, s, 0, 0))
    return pl.pallas_call(
        suffix_kernel,
        grid_spec=pltpu.PrefetchScalarGridSpec(
            num_scalar_prefetch=1,
            grid=(SLOTS,),
            in_specs=[pl.BlockSpec((1, KV, PER, W), lambda s, n: (s, 0, 0, 0)), wide, wide],
            out_specs=[out, out],
        ),
        out_shape=(shape, shape),
        compiler_params=params(16, 1),
        cost_estimate=pl.CostEstimate(
            flops=4 * SLOTS * HEADS * span * W, bytes_accessed=8 * MIB, transcendentals=SLOTS * HEADS * span
        ),
        name="suffix_attention",
    )(lengths, q, keys, values)


def prompt_kernel(q_ref, id_ref, k0, k1, v0, v1, out_ref, k_buf, v_buf, sems):
    step = pl.program_id(0)
    span = k0.shape[0]

    def copies():
        found = []
        for half, (k, v) in enumerate(((k0, v0), (k1, v1))):
            rows = pl.ds(half * span, span)
            found.append(pltpu.make_async_copy(k, k_buf.at[rows], sems.at[half]))
            for g in range(KV):
                found.append(
                    pltpu.make_async_copy(
                        v.at[:, pl.ds(g * W, W)],
                        v_buf.at[g, rows, pl.ds(0, W)],
                        sems.at[2 + 2 * half + g],
                    )
                )
        return found

    @pl.when(step == 0)
    def _():
        every = copies()
        for c in every:
            c.start()
        v_buf[:, :, W : 2 * W] = jnp.ones((KV, 2 * span, W), BF)
        for c in every:
            c.wait()

    lane = lax.broadcasted_iota(jnp.int32, (STEP * ROWS // KV, W), 1)
    marks = []
    for g in range(KV):
        half = ROWS // KV
        q = q_ref[:, g * half : (g + 1) * half, :].reshape(STEP * half, W)
        s = lax.dot_general(q, k_buf[:, g * W : (g + 1) * W], NT, preferred_element_type=F32)
        top = jnp.max(s, axis=1, keepdims=True) * TO_LOG2
        p = jnp.exp2(s * TO_LOG2 - top).astype(BF)
        o = jnp.dot(p, v_buf[g], preferred_element_type=F32)
        total = o[:, W:]
        out_ref[:, g * half : (g + 1) * half, :] = (o[:, :W] / total).astype(BF).reshape(STEP, half, W)
        lse = top + jnp.log2(total)
        high = lse.astype(BF).astype(F32)
        middle = (lse - high).astype(BF).astype(F32)
        low = (lse - high) - middle
        mark = jnp.where(lane == 0, high, jnp.where(lane == 1, middle, jnp.where(lane == 2, low, 0.0)))
        marks.append(mark.astype(BF).reshape(STEP, half, W))
    pick = (
        lax.broadcasted_iota(jnp.int32, (16, W), 0) == lax.broadcasted_iota(jnp.int32, (16, W), 1)
    ).astype(BF)
    for chip in range(STEP):
        column = jnp.concatenate([marks[0][chip], marks[1][chip], id_ref[...]], axis=0)
        row = lax.dot_general(pick, column, NT, preferred_element_type=F32)
        out_ref[chip, ROWS:PACKED, :] = row.astype(BF)


def prompt(q, ids, k0, k1, v0, v1):
    span = k0.shape[0]
    any_space = pl.BlockSpec(memory_space=pl.ANY)
    return pl.pallas_call(
        prompt_kernel,
        grid=(CHIPS // STEP,),
        in_specs=[
            pl.BlockSpec((STEP, ROWS, W), lambda i: (i, 0, 0)),
            pl.BlockSpec((W - ROWS, W), lambda i: (0, 0)),
            any_space,
            any_space,
            any_space,
            any_space,
        ],
        out_specs=pl.BlockSpec((STEP, PACKED, W), lambda i: (i, 0, 0)),
        out_shape=jax.ShapeDtypeStruct((CHIPS, PACKED, W), BF),
        scratch_shapes=[
            pltpu.VMEM((2 * span, KV * W), BF),
            pltpu.VMEM((KV, 2 * span, 2 * W), BF),
            pltpu.SemaphoreType.DMA((6,)),
        ],
        compiler_params=params(44, 1),
        cost_estimate=pl.CostEstimate(
            flops=4 * CHIPS * ROWS * 2 * span * W, bytes_accessed=6 * MIB, transcendentals=CHIPS * ROWS * 2 * span
        ),
        name="prompt_attention",
    )(q, ids, k0, k1, v0, v1)


def combine_kernel(part_ref, suffix_ref, suffix_lse_ref, out_ref):
    marks = part_ref[:, ROWS:PACKED, :].astype(F32)
    lse = marks[:, 0, :] + marks[:, 1, :] + marks[:, 2, :]
    lse = jnp.concatenate([lse, jnp.zeros((W - CHIPS, W), F32)], axis=0).T[:ROWS, :CHIPS]
    own = suffix_lse_ref[...]
    top = jnp.maximum(jnp.max(lse, axis=1, keepdims=True), own[:, :1])
    share = jnp.exp2(lse - top)
    own_share = jnp.exp2(own - top)
    total = jnp.sum(share, axis=1, keepdims=True) + own_share
    sums = [suffix_ref[...] * own_share] + [jnp.zeros((ROWS, W), F32)] * 3
    for chip in range(CHIPS):
        sums[chip % 4] += part_ref[chip, :ROWS, :].astype(F32) * share[:, chip : chip + 1]
    attention = (((sums[0] + sums[1]) + (sums[2] + sums[3])) / total).astype(BF)
    for chip in range(CHIPS):
        out_ref[chip] = attention


def combine(parts, suffix_out, suffix_lse):
    return pl.pallas_call(
        combine_kernel,
        out_shape=jax.ShapeDtypeStruct((CHIPS, ROWS, W), BF),
        compiler_params=params(8),
        name="combine_partials",
    )(parts, suffix_out, suffix_lse)


def project_kernel(core_ref, owner_ref, a_ref, w_own_ref, w_other_ref, out_ref, cat_ref):
    group = 4
    size = group * ROWS
    near = lax.broadcasted_iota(jnp.int32, (size, size), 0)
    far = lax.broadcasted_iota(jnp.int32, (size, size), 1)
    tall = group * SLOTS
    wanted = ((near % tall) // SLOTS) * ROWS + (near // tall) * SLOTS + near % SLOTS
    sort = (wanted == far).astype(BF)
    for i in range(CHIPS // group):
        rows = a_ref[i * group : (i + 1) * group].reshape(size, W)
        rows = jnp.dot(sort, rows, preferred_element_type=F32).astype(BF)
        for h in range(HEADS):
            cat_ref[i * tall : (i + 1) * tall, h * W : (h + 1) * W] = rows[h * tall : (h + 1) * tall, :]
    count = CHIPS * SLOTS
    samples = Y * CORES * SLOTS * CHIPS // Y
    ids = lax.broadcasted_iota(jnp.int32, (samples, count), 0)
    select = (ids == owner_ref[...]).astype(BF)
    core = core_ref[0]
    for which, w_ref in ((core, w_own_ref), (1 - core, w_other_ref)):
        projected = jnp.dot(cat_ref[...], w_ref[...], preferred_element_type=F32).astype(BF)
        placed = jnp.dot(select, projected, preferred_element_type=F32).astype(BF)
        out_ref[which] = placed.reshape(Y, samples // Y, W)


def project(core, owner, attention, w_own, w_other):
    vmem = pl.BlockSpec(memory_space=pltpu.VMEM)
    rows = CHIPS * SLOTS * CORES // Y
    return pl.pallas_call(
        project_kernel,
        in_specs=[pl.BlockSpec(memory_space=pltpu.SMEM), vmem, vmem, vmem, vmem],
        out_specs=vmem,
        out_shape=jax.ShapeDtypeStruct((CORES, Y, rows, W), BF),
        scratch_shapes=[pltpu.VMEM((CHIPS * SLOTS, HEADS * W), BF)],
        compiler_params=params(16),
        name="project",
    )(core, owner, attention, w_own, w_other)


def place(x, z, c):
    return (x * Z + z) * CORES + c


SAME_CORE = [[place(x, z, c) for x in range(X) for z in range(Z)] for c in range(CORES)]
OTHER_CORE = [(i, i ^ 1) for i in range(CHIPS * CORES)]
CORE_Y = [[place(x, z, c) * Y + y for c in range(CORES) for y in range(Y)] for x in range(X) for z in range(Z)]


def between_chips(a):
    return lax.all_to_all(a, "seq", 0, 0, axis_index_groups=SAME_CORE, tiled=True)


def on_device(queries, prompt_keys, prompt_values, keys, values, lengths, slot_sample, out_weight):
    other = functools.partial(lax.ppermute, axis_name="seq", perm=OTHER_CORE)
    gathered = between_chips(spread(queries))
    other_keys, other_values, other_weight = other(prompt_keys), other(prompt_values), other(out_weight)
    suffix_out, suffix_lse = suffix(
        lengths, queries.astype(F32).reshape(SLOTS, KV, PER, W), keys, values
    )
    suffix_out, suffix_lse = (
        a.transpose(0, 2, 1, 3).reshape(ROWS, W) for a in (suffix_out, suffix_lse)
    )
    ids = jnp.zeros((W - ROWS, W), BF).at[:SLOTS, 3].set(slot_sample.astype(BF))
    parts = prompt(gathered, ids, prompt_keys, other_keys, prompt_values, other_values)
    parts = between_chips(parts)
    owner = parts[:, ROWS + 3, ROWS : ROWS + SLOTS].astype(jnp.int32).reshape(1, CHIPS * SLOTS)
    attention = between_chips(combine(parts, suffix_out, suffix_lse))
    core = (lax.axis_index("seq") % CORES).astype(jnp.int32).reshape(1)
    placed = project(core, owner, attention, out_weight, other_weight)
    placed = placed.reshape(CORES * Y, placed.shape[2], W)
    placed = lax.all_to_all(placed, ("seq", "head"), 0, 0, axis_index_groups=CORE_Y, tiled=True)
    return placed.astype(F32).sum(axis=0).astype(BF)


def solution(mesh):
    return jax.shard_map(
        on_device,
        mesh=mesh,
        in_specs=(
            P("seq", "head"),
            P("seq", "head"),
            P("seq", "head"),
            P("seq", None, "head"),
            P("seq", None, "head"),
            P("seq"),
            P("seq"),
            P("head", "seq"),
        ),
        out_specs=P("head", "seq"),
        check_vma=False,
    )
```

```python
import functools

import jax
import jax.numpy as jnp
import numpy as np
from jax import lax
from jax.experimental import pallas as pl
from jax.experimental.pallas import tpu as pltpu
from jax.sharding import PartitionSpec as P

HEADS = 16
KV = 2
PER = 8
W = 128
SLOTS = 4
X, Z, CORES, Y = 4, 8, 2, 4
ROWS = HEADS * SLOTS
HALF = ROWS // KV
PACKED = ROWS + 16
CHUNK = 512
MIB = 1 << 20
BF, F32 = jnp.bfloat16, jnp.float32
TO_LOG2 = float(np.log2(np.e) * W**-0.5)
NT = (((1,), (1,)), ((), ()))


VMEM = pl.BlockSpec(memory_space=pltpu.VMEM)
HBM = pl.BlockSpec(memory_space=pltpu.HBM)


def params(limit):
    return pltpu.CompilerParams(vmem_limit_bytes=limit * MIB)


def spread_kernel(q_ref, out_ref, rows_ref):
    q = q_ref[...].astype(F32)
    rows = jnp.concatenate([q[:, h * W : (h + 1) * W] for h in range(HEADS)], axis=0)
    rows_ref[...] = rows
    block = rows.astype(BF)
    for chip in range(Z):
        out_ref[chip] = block


def spread(queries):
    return pl.pallas_call(
        spread_kernel,
        out_shape=(jax.ShapeDtypeStruct((Z, ROWS, W), BF), jax.ShapeDtypeStruct((ROWS, W), F32)),
        compiler_params=params(8),
        name="spread_queries",
    )(queries)


def suffix_kernel(length_ref, q_ref, k_ref, v_ref, out_ref, lse_ref, k_buf, v_buf, sems):
    span = k_ref.shape[1]
    copies = []
    for slot in range(SLOTS):
        for i, (ref, buf) in enumerate(((k_ref, k_buf), (v_ref, v_buf))):
            copies.append(pltpu.make_async_copy(ref.at[slot], buf.at[slot], sems.at[2 * slot + i]))
            copies[-1].start()
    at = lax.broadcasted_iota(jnp.int32, (PER, span), 1)
    for slot in range(SLOTS):
        copies[2 * slot].wait()
        scores = []
        for g in range(KV):
            keys = k_buf[slot, :, g * W : (g + 1) * W]
            s = lax.dot_general(q_ref[pl.ds(g * HALF + slot, PER, SLOTS), :].astype(BF), keys, NT, preferred_element_type=F32)
            scores.append(jnp.where(at < length_ref[slot], s * TO_LOG2, -1e30))
        copies[2 * slot + 1].wait()
        for g in range(KV):
            top = jnp.max(scores[g], axis=1, keepdims=True)
            p = jnp.exp2(scores[g] - top)
            total = jnp.sum(p, axis=1, keepdims=True)
            values = v_buf[slot, :, g * W : (g + 1) * W]
            o = jnp.dot(p.astype(BF), values, preferred_element_type=F32)
            rows = pl.ds(g * HALF + slot, PER, SLOTS)
            out_ref[rows, :] = o / total
            lse_ref[rows, :] = jnp.broadcast_to(top + jnp.log2(total), (PER, W))


def suffix(lengths, q, keys, values):
    shape = jax.ShapeDtypeStruct((ROWS, W), F32)
    return pl.pallas_call(
        suffix_kernel,
        in_specs=[pl.BlockSpec(memory_space=pltpu.SMEM), VMEM, HBM, HBM],
        out_specs=(VMEM, VMEM),
        out_shape=(shape, shape),
        scratch_shapes=[
            pltpu.VMEM(keys.shape, BF),
            pltpu.VMEM(keys.shape, BF),
            pltpu.SemaphoreType.DMA((2 * SLOTS,)),
        ],
        compiler_params=params(58),
        cost_estimate=pl.CostEstimate(
            flops=4 * HEADS * W * keys.shape[0] * keys.shape[1],
            bytes_accessed=8 * MIB,
            transcendentals=SLOTS * HEADS * keys.shape[1],
        ),
        name="suffix_attention",
    )(lengths, q, keys, values)


def pieces(lse):
    high = lse.astype(BF).astype(F32)
    middle = (lse - high).astype(BF).astype(F32)
    return high, middle, (lse - high) - middle


def prompt_kernel(count, *refs):
    q_refs, (k0, k1, v0, v1) = refs[:count], refs[count : count + 4]
    out_refs, (k_buf, v_buf, sems) = refs[count + 4 : 2 * count + 4], refs[2 * count + 4 :]
    span = k0.shape[0]
    waits = [{}, {}, {}]
    for i, (k, v) in enumerate(((k0, v0), (k1, v1))):
        rows = pl.ds(i * span, span)
        waits[0][i * span] = pltpu.make_async_copy(k, k_buf.at[rows], sems.at[3 * i])
        for g in range(KV):
            target = v_buf.at[g, rows, pl.ds(0, W)]
            source = v.at[:, pl.ds(g * W, W)]
            waits[1 + g][i * span] = pltpu.make_async_copy(source, target, sems.at[3 * i + 1 + g])
        for wait in waits:
            wait[i * span].start()
    v_buf[:, :, W:] = jnp.ones((KV, 2 * span, W), BF)

    total_rows = count * Z * HALF
    lane = lax.broadcasted_iota(jnp.int32, (total_rows, W), 1)
    marks = []
    for g in range(KV):
        q = [ref[:, g * HALF : (g + 1) * HALF, :].reshape(Z * HALF, W) for ref in q_refs]
        q = jnp.concatenate(q, axis=0) if count > 1 else q[0]
        top = jnp.full((total_rows, 1), -1e30, F32)
        o = jnp.zeros((total_rows, 2 * W), F32)
        for at in range(0, 2 * span, CHUNK):
            if at in waits[0]:
                waits[0].pop(at).wait()
            keys = k_buf[at : at + CHUNK, g * W : (g + 1) * W]
            s = lax.dot_general(q, keys, NT, preferred_element_type=F32)
            new = jnp.maximum(top, jnp.max(s, axis=1, keepdims=True) * TO_LOG2)
            p = jnp.exp2(s * TO_LOG2 - new).astype(BF)
            if at in waits[1 + g]:
                waits[1 + g].pop(at).wait()
            o = o * jnp.exp2(top - new) + jnp.dot(p, v_buf[g, at : at + CHUNK, :], preferred_element_type=F32)
            top = new
        total = o[:, W:]
        mean = (o[:, :W] / total).astype(BF).reshape(count, Z, HALF, W)
        for i, out_ref in enumerate(out_refs):
            out_ref[:, g * HALF : (g + 1) * HALF, :] = mean[i]
        high, middle, low = pieces(top + jnp.log2(total))
        mark = jnp.where(lane == 0, high, jnp.where(lane == 1, middle, jnp.where(lane == 2, low, 0.0)))
        marks.append(mark.astype(BF).reshape(count, Z, HALF, W))
    pick = (
        lax.broadcasted_iota(jnp.int32, (16, W), 0) == lax.broadcasted_iota(jnp.int32, (16, W), 1)
    ).astype(BF)
    nothing = jnp.zeros((W - ROWS, W), BF)
    for i, out_ref in enumerate(out_refs):
        for z in range(Z):
            column = jnp.concatenate([marks[0][i, z], marks[1][i, z], nothing], axis=0)
            row = lax.dot_general(pick, column, NT, preferred_element_type=F32)
            out_ref[z, ROWS:PACKED, :] = row.astype(BF)


def prompt(qs, ks, vs, name):
    count, span = len(qs), 2 * ks[0].shape[0]
    out = jax.ShapeDtypeStruct((Z, PACKED, W), BF)
    return pl.pallas_call(
        functools.partial(prompt_kernel, count),
        in_specs=[VMEM] * count + [HBM] * 4,
        out_specs=[VMEM] * count,
        out_shape=[out] * count,
        scratch_shapes=[
            pltpu.VMEM((span, KV * W), BF),
            pltpu.VMEM((KV, span, 2 * W), BF),
            pltpu.SemaphoreType.DMA((6,)),
        ],
        compiler_params=params(40),
        cost_estimate=pl.CostEstimate(
            flops=4 * count * Z * ROWS * span * W,
            bytes_accessed=5 * MIB,
            transcendentals=count * Z * ROWS * span,
        ),
        name=name,
    )(*qs, *ks, *vs)


def lse_rows(ref):
    marks = ref[:, ROWS:PACKED, :].astype(F32)
    return marks[:, 0, :] + marks[:, 1, :] + marks[:, 2, :]


def turned(rows):
    return jnp.concatenate([rows, jnp.zeros((W - rows.shape[0], W), F32)], axis=0).T[:ROWS]


def merge_kernel(p0, p1, p2, p3, id_ref, out_ref):
    parts = (p0, p1, p2, p3)
    lses = [lse_rows(p) for p in parts]
    top = functools.reduce(jnp.maximum, lses)
    shares = [jnp.exp2(lse - top) for lse in lses]
    total = functools.reduce(jnp.add, shares)
    columns = turned(jnp.concatenate([share / total for share in shares], axis=0))
    new = pieces(top + jnp.log2(total))
    row = lax.broadcasted_iota(jnp.int32, (16, W), 0)
    for z in range(Z):
        terms = [
            p[z, :ROWS, :].astype(F32) * columns[:, i * Z + z : i * Z + z + 1] for i, p in enumerate(parts)
        ]
        out_ref[z, :ROWS, :] = ((terms[0] + terms[1]) + (terms[2] + terms[3])).astype(BF)
        tile = jnp.where(row == 3, id_ref[...], 0.0)
        for i, piece in enumerate(new):
            tile = jnp.where(row == i, piece[z : z + 1, :], tile)
        out_ref[z, ROWS:PACKED, :] = tile.astype(BF)


def merge(parts, ids):
    return pl.pallas_call(
        merge_kernel,
        out_shape=jax.ShapeDtypeStruct((Z, PACKED, W), BF),
        compiler_params=params(8),
        name="merge_along_x",
    )(*parts, ids)


def combine_kernel(part_ref, suffix_ref, suffix_lse_ref, out_ref):
    lse = turned(lse_rows(part_ref))[:, :Z]
    own = suffix_lse_ref[...]
    top = jnp.maximum(jnp.max(lse, axis=1, keepdims=True), jnp.max(own, axis=1, keepdims=True))
    share = jnp.exp2(lse - top)
    own_share = jnp.exp2(own - top)
    total = jnp.sum(share, axis=1, keepdims=True) + own_share
    sums = [suffix_ref[...] * own_share, jnp.zeros((ROWS, W), F32)]
    for z in range(Z):
        sums[z % 2] += part_ref[z, :ROWS, :].astype(F32) * share[:, z : z + 1]
    attention = ((sums[0] + sums[1]) / total).astype(BF)
    for z in range(Z):
        out_ref[z] = attention


def combine(parts, suffix_out, suffix_lse):
    return pl.pallas_call(
        combine_kernel,
        out_shape=jax.ShapeDtypeStruct((Z, ROWS, W), BF),
        compiler_params=params(8),
        name="combine_along_z",
    )(parts, suffix_out, suffix_lse)


def tick_kernel(in_ref, out_ref):
    out_ref[...] = in_ref[...]


def tick(a):
    return pl.pallas_call(
        tick_kernel,
        out_shape=jax.ShapeDtypeStruct(a.shape, a.dtype),
        compiler_params=params(8),
        cost_estimate=pl.CostEstimate(flops=0, bytes_accessed=4 * MIB, transcendentals=0),
        name="tick",
    )(a)


def project_kernel(at_ref, a_ref, b_ref, id_ref, *refs):
    w_refs, (out_ref, cat_ref) = refs[:X], refs[X:]
    group = 4
    size = group * ROWS
    near = lax.broadcasted_iota(jnp.int32, (size, size), 0)
    far = lax.broadcasted_iota(jnp.int32, (size, size), 1)
    tall = group * SLOTS
    wanted = ((near % tall) // SLOTS) * ROWS + (near // tall) * SLOTS + near % SLOTS
    sort = (wanted == far).astype(BF)
    for i in range(CORES * Z // group):
        half, first = divmod(i * group, Z)
        rows = (a_ref, b_ref)[half][first : first + group].reshape(size, W)
        rows = jnp.dot(sort, rows, preferred_element_type=F32).astype(BF)
        for h in range(HEADS):
            cat_ref[i * tall : (i + 1) * tall, h * W : (h + 1) * W] = rows[h * tall : (h + 1) * tall, :]
    count = CORES * Z * SLOTS
    for block, w_ref in enumerate(w_refs):
        projected = jnp.dot(cat_ref[...], w_ref[...], preferred_element_type=F32).astype(BF)
        to = lax.rem(at_ref[0] + block, X) * Y
        for y in range(Y):
            out_ref[to + y, :count, :] = projected
            out_ref[to + y, count:, :] = id_ref[...]


def project(at, own, others, ids, weights):
    count = CORES * Z * SLOTS
    return pl.pallas_call(
        project_kernel,
        in_specs=[pl.BlockSpec(memory_space=pltpu.SMEM)] + [VMEM] * (3 + len(weights)),
        out_specs=VMEM,
        out_shape=jax.ShapeDtypeStruct((X * Y, count + 16, W), BF),
        scratch_shapes=[pltpu.VMEM((count, HEADS * W), BF)],
        compiler_params=params(16),
        name="project",
    )(at, own, others, ids, *weights)


def finish_kernel(at_ref, part_ref, out_ref):
    count = CORES * Z * SLOTS
    ids = lax.broadcasted_iota(jnp.int32, (out_ref.shape[0], W), 0) + at_ref[1] * out_ref.shape[0]
    result = jnp.zeros(out_ref.shape, F32)
    for block in range(X):
        part = [part_ref[block * Y + y, :count, :].astype(F32) for y in range(Y)]
        rows = ((part[0] + part[1]) + (part[2] + part[3])).astype(BF)
        owner = part_ref[block * Y, count:, :].astype(F32)[:1, :].astype(jnp.int32)
        select = (ids == owner).astype(BF)[:, :count]
        result += jnp.dot(select, rows, preferred_element_type=F32)
    out_ref[...] = result.astype(BF)


def finish(at, parts):
    return pl.pallas_call(
        finish_kernel,
        in_specs=[pl.BlockSpec(memory_space=pltpu.SMEM), VMEM],
        out_specs=VMEM,
        out_shape=jax.ShapeDtypeStruct((X * CORES * Z * SLOTS // Y, W), BF),
        compiler_params=params(8),
        name="finish",
    )(at, parts)


def place(x, z, c):
    return (x * Z + z) * CORES + c


OTHER_CORE = [(i, i ^ 1) for i in range(X * Z * CORES)]
ALONG_Z = [[place(x, z, c) for z in range(Z)] for x in range(X) for c in range(CORES)]
X_Y = [
    [place(x, z, c) * Y + y for x in range(X) for y in range(Y)] for z in range(Z) for c in range(CORES)
]


def other(a):
    return lax.ppermute(a, "seq", OTHER_CORE)


def shift(a, by):
    pairs = [
        (place(x, z, c), place((x + by) % X, z, c)) for x in range(X) for z in range(Z) for c in range(CORES)
    ]
    return lax.ppermute(a, "seq", pairs)


def exchange(a, groups, axes="seq"):
    return lax.all_to_all(a, axes, 0, 0, axis_index_groups=groups, tiled=True)


def on_device(queries, prompt_keys, prompt_values, keys, values, lengths, slot_sample, out_weight):
    after = lax.optimization_barrier
    at = jnp.stack([lax.axis_index("seq") // (Z * CORES), lax.axis_index("head")]).astype(jnp.int32)
    block, rows = spread(queries)
    block, prompt_keys, prompt_values, out_weight = after((block, prompt_keys, prompt_values, out_weight))
    own = exchange(block, ALONG_Z)
    ks, vs = (prompt_keys, other(prompt_keys)), (prompt_values, other(prompt_values))
    weights = {0: out_weight, 1: shift(out_weight, -1), 3: shift(out_weight, 1)}
    own, weights[1], weights[3] = after((own, weights[1], weights[3]))
    away = [shift(own, -d) for d in range(1, X)]
    (own_part,) = prompt([own], ks, vs, "prompt_own")
    own_part, *away = after((own_part, *away))
    away_parts = prompt(away, ks, vs, "prompt_away")
    *away_parts, rows = after((*away_parts, rows))
    away_parts = [shift(a, d) for d, a in zip(range(1, X), away_parts)]
    suffix_out, suffix_lse = suffix(lengths, rows, keys, values)
    suffix_out, suffix_lse, *away_parts = after((suffix_out, suffix_lse, *away_parts))
    ids = jnp.pad(slot_sample.astype(F32), (ROWS, W - ROWS - SLOTS)).reshape(1, W)
    merged = merge([own_part, *away_parts], ids)
    merged, mark = after((merged, at))
    parts = exchange(merged, ALONG_Z)
    mark, weight = after((tick(mark.reshape(1, -1)), out_weight))
    weights[2] = shift(weight, 2)
    attention = exchange(combine(parts, suffix_out, suffix_lse), ALONG_Z)
    owner = parts[:, ROWS + 3, ROWS : ROWS + SLOTS].reshape(1, Z * SLOTS)
    owner = jnp.concatenate([owner, other(jnp.broadcast_to(owner, (8, Z * SLOTS)))[:1]], axis=1)
    owner = jnp.pad(owner, ((0, 15), (0, W - CORES * Z * SLOTS)))
    placed = project(at, attention, other(attention), owner, [weights[d] for d in range(X)])
    return finish(at, exchange(placed, X_Y, ("seq", "head")))


def solution(mesh):
    return jax.shard_map(
        on_device,
        mesh=mesh,
        in_specs=(
            P("seq", "head"),
            P("seq", "head"),
            P("seq", "head"),
            P("seq", None, "head"),
            P("seq", None, "head"),
            P("seq"),
            P("seq"),
            P("head", "seq"),
        ),
        out_specs=P("head", "seq"),
        check_vma=False,
    )
```

```python
import functools

import jax
import jax.numpy as jnp
import numpy as np
from jax import lax
from jax.experimental import pallas as pl
from jax.experimental.pallas import tpu as pltpu
from jax.sharding import PartitionSpec as P

HEADS = 16
KV = 2
PER = 8
W = 128
SLOTS = 4
X, Z, CORES, Y = 4, 8, 2, 4
ROWS = HEADS * SLOTS
HALF = ROWS // KV
PACKED = ROWS + 16
CHUNK = 512
MIB = 1 << 20
BF, F32 = jnp.bfloat16, jnp.float32
TO_LOG2 = float(np.log2(np.e) * W**-0.5)
NT = (((1,), (1,)), ((), ()))


VMEM = pl.BlockSpec(memory_space=pltpu.VMEM)
HBM = pl.BlockSpec(memory_space=pltpu.HBM)


def params(limit):
    return pltpu.CompilerParams(vmem_limit_bytes=limit * MIB)


def spread_kernel(q_ref, out_ref, rows_ref):
    q = q_ref[...].astype(F32)
    rows = jnp.concatenate([q[:, h * W : (h + 1) * W] for h in range(HEADS)], axis=0)
    rows_ref[...] = rows
    block = rows.astype(BF)
    for chip in range(Z):
        out_ref[chip] = block


def spread(queries):
    return pl.pallas_call(
        spread_kernel,
        out_shape=(jax.ShapeDtypeStruct((Z, ROWS, W), BF), jax.ShapeDtypeStruct((ROWS, W), F32)),
        compiler_params=params(8),
        name="spread_queries",
    )(queries)


def suffix_kernel(length_ref, q_ref, k_ref, v_ref, out_ref, lse_ref, k_buf, v_buf, sems):
    span = k_ref.shape[1]
    copies = []
    for slot in range(SLOTS):
        for i, (ref, buf) in enumerate(((k_ref, k_buf), (v_ref, v_buf))):
            copies.append(pltpu.make_async_copy(ref.at[slot], buf.at[slot], sems.at[2 * slot + i]))
            copies[-1].start()
    at = lax.broadcasted_iota(jnp.int32, (PER, span), 1)
    for slot in range(SLOTS):
        copies[2 * slot].wait()
        scores = []
        for g in range(KV):
            keys = k_buf[slot, :, g * W : (g + 1) * W]
            s = lax.dot_general(q_ref[pl.ds(g * HALF + slot, PER, SLOTS), :].astype(BF), keys, NT, preferred_element_type=F32)
            scores.append(jnp.where(at < length_ref[slot], s * TO_LOG2, -1e30))
        copies[2 * slot + 1].wait()
        for g in range(KV):
            top = jnp.max(scores[g], axis=1, keepdims=True)
            p = jnp.exp2(scores[g] - top)
            total = jnp.sum(p, axis=1, keepdims=True)
            values = v_buf[slot, :, g * W : (g + 1) * W]
            o = jnp.dot(p.astype(BF), values, preferred_element_type=F32)
            rows = pl.ds(g * HALF + slot, PER, SLOTS)
            out_ref[rows, :] = o / total
            lse_ref[rows, :] = jnp.broadcast_to(top + jnp.log2(total), (PER, W))


def suffix(lengths, q, keys, values):
    shape = jax.ShapeDtypeStruct((ROWS, W), F32)
    return pl.pallas_call(
        suffix_kernel,
        in_specs=[pl.BlockSpec(memory_space=pltpu.SMEM), VMEM, HBM, HBM],
        out_specs=(VMEM, VMEM),
        out_shape=(shape, shape),
        scratch_shapes=[
            pltpu.VMEM(keys.shape, BF),
            pltpu.VMEM(keys.shape, BF),
            pltpu.SemaphoreType.DMA((2 * SLOTS,)),
        ],
        compiler_params=params(58),
        cost_estimate=pl.CostEstimate(
            flops=4 * HEADS * W * keys.shape[0] * keys.shape[1],
            bytes_accessed=8 * MIB,
            transcendentals=SLOTS * HEADS * keys.shape[1],
        ),
        name="suffix_attention",
    )(lengths, q, keys, values)


def pieces(lse):
    high = lse.astype(BF).astype(F32)
    middle = (lse - high).astype(BF).astype(F32)
    return high, middle, (lse - high) - middle


def prompt_kernel(count, *refs):
    q_refs, (k0, k1, v0, v1) = refs[:count], refs[count : count + 4]
    out_refs, v_buf = refs[count + 4 : 2 * count + 4], refs[2 * count + 4]
    span = k0.shape[0]
    for half, v in enumerate((v0, v1)):
        for g in range(KV):
            v_buf[g, half * span : (half + 1) * span, :W] = v[:, g * W : (g + 1) * W]
    v_buf[:, :, W:] = jnp.ones((KV, 2 * span, W), BF)

    total_rows = count * Z * HALF
    lane = lax.broadcasted_iota(jnp.int32, (total_rows, W), 1)
    marks = []
    for g in range(KV):
        q = [ref[:, g * HALF : (g + 1) * HALF, :].reshape(Z * HALF, W) for ref in q_refs]
        q = jnp.concatenate(q, axis=0) if count > 1 else q[0]
        top = jnp.full((total_rows, 1), -1e30, F32)
        o = jnp.zeros((total_rows, 2 * W), F32)
        for at in range(0, 2 * span, CHUNK):
            keys = (k0, k1)[at // span][at % span : at % span + CHUNK, g * W : (g + 1) * W]
            s = lax.dot_general(q, keys, NT, preferred_element_type=F32)
            new = jnp.maximum(top, jnp.max(s, axis=1, keepdims=True) * TO_LOG2)
            p = jnp.exp2(s * TO_LOG2 - new).astype(BF)
            o = o * jnp.exp2(top - new) + jnp.dot(p, v_buf[g, at : at + CHUNK, :], preferred_element_type=F32)
            top = new
        total = o[:, W:]
        mean = (o[:, :W] / total).astype(BF).reshape(count, Z, HALF, W)
        for i, out_ref in enumerate(out_refs):
            out_ref[:, g * HALF : (g + 1) * HALF, :] = mean[i]
        high, middle, low = pieces(top + jnp.log2(total))
        mark = jnp.where(lane == 0, high, jnp.where(lane == 1, middle, jnp.where(lane == 2, low, 0.0)))
        marks.append(mark.astype(BF).reshape(count, Z, HALF, W))
    pick = (
        lax.broadcasted_iota(jnp.int32, (16, W), 0) == lax.broadcasted_iota(jnp.int32, (16, W), 1)
    ).astype(BF)
    nothing = jnp.zeros((W - ROWS, W), BF)
    for i, out_ref in enumerate(out_refs):
        for z in range(Z):
            column = jnp.concatenate([marks[0][i, z], marks[1][i, z], nothing], axis=0)
            row = lax.dot_general(pick, column, NT, preferred_element_type=F32)
            out_ref[z, ROWS:PACKED, :] = row.astype(BF)


def prompt(qs, ks, vs, name):
    count, span = len(qs), 2 * ks[0].shape[0]
    out = jax.ShapeDtypeStruct((Z, PACKED, W), BF)
    return pl.pallas_call(
        functools.partial(prompt_kernel, count),
        out_shape=[out] * count,
        scratch_shapes=[pltpu.VMEM((KV, span, 2 * W), BF)],
        compiler_params=params(32),
        cost_estimate=pl.CostEstimate(
            flops=4 * count * Z * ROWS * span * W,
            bytes_accessed=5 * MIB,
            transcendentals=count * Z * ROWS * span,
        ),
        name=name,
    )(*qs, *ks, *vs)


def lse_rows(ref):
    marks = ref[:, ROWS:PACKED, :].astype(F32)
    return marks[:, 0, :] + marks[:, 1, :] + marks[:, 2, :]


def turned(rows):
    return jnp.concatenate([rows, jnp.zeros((W - rows.shape[0], W), F32)], axis=0).T[:ROWS]


def merge_kernel(id_ref, p0, p1, p2, p3, out_ref):
    parts = (p0, p1, p2, p3)
    lses = [lse_rows(p) for p in parts]
    top = functools.reduce(jnp.maximum, lses)
    shares = [jnp.exp2(lse - top) for lse in lses]
    total = functools.reduce(jnp.add, shares)
    columns = turned(jnp.concatenate([share / total for share in shares], axis=0))
    new = pieces(top + jnp.log2(total))
    row = lax.broadcasted_iota(jnp.int32, (16, W), 0)
    lane = lax.broadcasted_iota(jnp.int32, (16, W), 1)
    ids = jnp.zeros((16, W), jnp.int32)
    for slot in range(SLOTS):
        ids = jnp.where((row == 3) & (lane == ROWS + slot), id_ref[slot], ids)
    ids = ids.astype(F32)
    for z in range(Z):
        terms = [
            p[z, :ROWS, :].astype(F32) * columns[:, i * Z + z : i * Z + z + 1] for i, p in enumerate(parts)
        ]
        out_ref[z, :ROWS, :] = ((terms[0] + terms[1]) + (terms[2] + terms[3])).astype(BF)
        tile = ids
        for i, piece in enumerate(new):
            tile = jnp.where(row == i, piece[z : z + 1, :], tile)
        out_ref[z, ROWS:PACKED, :] = tile.astype(BF)


def merge(ids, parts):
    return pl.pallas_call(
        merge_kernel,
        in_specs=[pl.BlockSpec(memory_space=pltpu.SMEM)] + [VMEM] * X,
        out_specs=VMEM,
        out_shape=jax.ShapeDtypeStruct((Z, PACKED, W), BF),
        compiler_params=params(8),
        name="merge_along_x",
    )(ids, *parts)


def combine_kernel(part_ref, suffix_ref, suffix_lse_ref, out_ref):
    lse = turned(lse_rows(part_ref))[:, :Z]
    own = suffix_lse_ref[...]
    top = jnp.maximum(jnp.max(lse, axis=1, keepdims=True), jnp.max(own, axis=1, keepdims=True))
    share = jnp.exp2(lse - top)
    own_share = jnp.exp2(own - top)
    total = jnp.sum(share, axis=1, keepdims=True) + own_share
    sums = [suffix_ref[...] * own_share, jnp.zeros((ROWS, W), F32)]
    for z in range(Z):
        sums[z % 2] += part_ref[z, :ROWS, :].astype(F32) * share[:, z : z + 1]
    attention = ((sums[0] + sums[1]) / total).astype(BF)
    for z in range(Z):
        out_ref[z] = attention


def combine(parts, suffix_out, suffix_lse):
    return pl.pallas_call(
        combine_kernel,
        out_shape=jax.ShapeDtypeStruct((Z, ROWS, W), BF),
        compiler_params=params(8),
        name="combine_along_z",
    )(parts, suffix_out, suffix_lse)


def tick_kernel(a_ref, b_ref, c_ref, d_ref):
    c_ref[...] = a_ref[...]
    d_ref[...] = b_ref[...]


def tick(a, b):
    return pl.pallas_call(
        tick_kernel,
        out_shape=tuple(jax.ShapeDtypeStruct(x.shape, x.dtype) for x in (a, b)),
        compiler_params=params(8),
        cost_estimate=pl.CostEstimate(flops=0, bytes_accessed=4 * MIB, transcendentals=0),
        name="bring_suffix",
    )(a, b)


def project_kernel(at_ref, a_ref, b_ref, id_ref, *refs):
    w_refs, (out_ref, cat_ref) = refs[:X], refs[X:]
    group = 4
    size = group * ROWS
    near = lax.broadcasted_iota(jnp.int32, (size, size), 0)
    far = lax.broadcasted_iota(jnp.int32, (size, size), 1)
    tall = group * SLOTS
    wanted = ((near % tall) // SLOTS) * ROWS + (near // tall) * SLOTS + near % SLOTS
    sort = (wanted == far).astype(BF)
    for i in range(CORES * Z // group):
        half, first = divmod(i * group, Z)
        rows = (a_ref, b_ref)[half][first : first + group].reshape(size, W)
        rows = jnp.dot(sort, rows, preferred_element_type=F32).astype(BF)
        for h in range(HEADS):
            cat_ref[i * tall : (i + 1) * tall, h * W : (h + 1) * W] = rows[h * tall : (h + 1) * tall, :]
    count = CORES * Z * SLOTS
    for block, w_ref in enumerate(w_refs):
        projected = jnp.dot(cat_ref[...], w_ref[...], preferred_element_type=F32).astype(BF)
        to = lax.rem(at_ref[0] + block, X) * Y
        for y in range(Y):
            out_ref[to + y, :count, :] = projected
            out_ref[to + y, count:, :] = id_ref[...]


def project(at, own, others, ids, weights):
    count = CORES * Z * SLOTS
    return pl.pallas_call(
        project_kernel,
        in_specs=[pl.BlockSpec(memory_space=pltpu.SMEM)] + [VMEM] * (3 + len(weights)),
        out_specs=VMEM,
        out_shape=jax.ShapeDtypeStruct((X * Y, count + 16, W), BF),
        scratch_shapes=[pltpu.VMEM((count, HEADS * W), BF)],
        compiler_params=params(16),
        name="project",
    )(at, own, others, ids, *weights)


def finish_kernel(at_ref, part_ref, out_ref):
    count = CORES * Z * SLOTS
    ids = lax.broadcasted_iota(jnp.int32, (out_ref.shape[0], W), 0) + at_ref[1] * out_ref.shape[0]
    result = jnp.zeros(out_ref.shape, F32)
    for block in range(X):
        part = [part_ref[block * Y + y, :count, :].astype(F32) for y in range(Y)]
        rows = ((part[0] + part[1]) + (part[2] + part[3])).astype(BF)
        owner = part_ref[block * Y, count:, :].astype(F32)[:1, :].astype(jnp.int32)
        select = (ids == owner).astype(BF)[:, :count]
        result += jnp.dot(select, rows, preferred_element_type=F32)
    out_ref[...] = result.astype(BF)


def finish(at, parts):
    return pl.pallas_call(
        finish_kernel,
        in_specs=[pl.BlockSpec(memory_space=pltpu.SMEM), VMEM],
        out_specs=VMEM,
        out_shape=jax.ShapeDtypeStruct((X * CORES * Z * SLOTS // Y, W), BF),
        compiler_params=params(8),
        name="finish",
    )(at, parts)


def place(x, z, c):
    return (x * Z + z) * CORES + c


OTHER_CORE = [(i, i ^ 1) for i in range(X * Z * CORES)]
ALONG_Z = [[place(x, z, c) for z in range(Z)] for x in range(X) for c in range(CORES)]
X_Y = [
    [place(x, z, c) * Y + y for x in range(X) for y in range(Y)] for z in range(Z) for c in range(CORES)
]


def other(a):
    return lax.ppermute(a, "seq", OTHER_CORE)


def shift(a, by):
    pairs = [
        (place(x, z, c), place((x + by) % X, z, c)) for x in range(X) for z in range(Z) for c in range(CORES)
    ]
    return lax.ppermute(a, "seq", pairs)


def exchange(a, groups, axes="seq"):
    return lax.all_to_all(a, axes, 0, 0, axis_index_groups=groups, tiled=True)


def on_device(queries, prompt_keys, prompt_values, keys, values, lengths, slot_sample, out_weight):
    after = lax.optimization_barrier
    at = jnp.stack([lax.axis_index("seq") // (Z * CORES), lax.axis_index("head")]).astype(jnp.int32)
    block, rows = spread(queries)
    block, prompt_keys, prompt_values, out_weight = after((block, prompt_keys, prompt_values, out_weight))
    own = exchange(block, ALONG_Z)
    ks, vs = (prompt_keys, other(prompt_keys)), (prompt_values, other(prompt_values))
    weights = {0: out_weight, 1: shift(out_weight, -1), 3: shift(out_weight, 1)}
    away = [shift(own, -d) for d in range(1, X)]
    (own_part,) = prompt([own], ks, vs, "prompt_own")
    own_part, weights[1], weights[3], *away = after((own_part, weights[1], weights[3], *away))
    away_parts = prompt(away, ks, vs, "prompt_away")
    *away_parts, rows = after((*away_parts, rows))
    away_parts = [shift(a, d) for d, a in zip(range(1, X), away_parts)]
    suffix_out, suffix_lse = suffix(lengths, rows, keys, values)
    suffix_out, suffix_lse, *away_parts = after((suffix_out, suffix_lse, *away_parts))
    merged = merge(slot_sample, [own_part, *away_parts])
    merged, suffix_out, suffix_lse = after((merged, suffix_out, suffix_lse))
    parts = exchange(merged, ALONG_Z)
    suffix_out, suffix_lse, weight = after((*tick(suffix_out, suffix_lse), out_weight))
    weights[2] = shift(weight, 2)
    attention = exchange(combine(parts, suffix_out, suffix_lse), ALONG_Z)
    owner = parts[:, ROWS + 3, ROWS : ROWS + SLOTS].reshape(1, Z * SLOTS)
    owner = jnp.concatenate([owner, other(jnp.broadcast_to(owner, (8, Z * SLOTS)))[:1]], axis=1)
    owner = jnp.pad(owner, ((0, 15), (0, W - CORES * Z * SLOTS)))
    placed = project(at, attention, other(attention), owner, [weights[d] for d in range(X)])
    return finish(at, exchange(placed, X_Y, ("seq", "head")))


def solution(mesh):
    return jax.shard_map(
        on_device,
        mesh=mesh,
        in_specs=(
            P("seq", "head"),
            P("seq", "head"),
            P("seq", "head"),
            P("seq", None, "head"),
            P("seq", None, "head"),
            P("seq"),
            P("seq"),
            P("head", "seq"),
        ),
        out_specs=P("head", "seq"),
        check_vma=False,
    )
```

```python
import functools

import jax
import jax.numpy as jnp
import numpy as np
from jax import lax
from jax.experimental import pallas as pl
from jax.experimental.pallas import tpu as pltpu
from jax.sharding import PartitionSpec as P

HEADS = 16
KV = 2
PER = 8
W = 128
SLOTS = 4
X, Z, CORES, Y = 4, 8, 2, 4
ROWS = HEADS * SLOTS
HALF = ROWS // KV
PACKED = ROWS + 16
CHUNK = 512
MIB = 1 << 20
BF, F32 = jnp.bfloat16, jnp.float32
TO_LOG2 = float(np.log2(np.e) * W**-0.5)
NT = (((1,), (1,)), ((), ()))


VMEM = pl.BlockSpec(memory_space=pltpu.VMEM)
HBM = pl.BlockSpec(memory_space=pltpu.HBM)


def params(limit):
    return pltpu.CompilerParams(vmem_limit_bytes=limit * MIB)


def spread_kernel(q_ref, out_ref, rows_ref):
    q = q_ref[...].astype(F32)
    rows = jnp.concatenate([q[:, h * W : (h + 1) * W] for h in range(HEADS)], axis=0)
    rows_ref[...] = rows
    block = rows.astype(BF)
    for chip in range(Z):
        out_ref[chip] = block


def spread(queries):
    return pl.pallas_call(
        spread_kernel,
        out_shape=(jax.ShapeDtypeStruct((Z, ROWS, W), BF), jax.ShapeDtypeStruct((ROWS, W), F32)),
        compiler_params=params(8),
        name="spread_queries",
    )(queries)


def suffix_kernel(length_ref, q_ref, k_ref, v_ref, out_ref, lse_ref, k_buf, v_buf, sems):
    span = k_ref.shape[1]
    copies = []
    for slot in range(SLOTS):
        for i, (ref, buf) in enumerate(((k_ref, k_buf), (v_ref, v_buf))):
            copies.append(pltpu.make_async_copy(ref.at[slot], buf.at[slot], sems.at[2 * slot + i]))
            copies[-1].start()
    at = lax.broadcasted_iota(jnp.int32, (PER, span), 1)
    for slot in range(SLOTS):
        copies[2 * slot].wait()
        scores = []
        for g in range(KV):
            keys = k_buf[slot, :, g * W : (g + 1) * W]
            s = lax.dot_general(q_ref[pl.ds(g * HALF + slot, PER, SLOTS), :].astype(BF), keys, NT, preferred_element_type=F32)
            scores.append(jnp.where(at < length_ref[slot], s * TO_LOG2, -1e30))
        copies[2 * slot + 1].wait()
        for g in range(KV):
            top = jnp.max(scores[g], axis=1, keepdims=True)
            p = jnp.exp2(scores[g] - top)
            total = jnp.sum(p, axis=1, keepdims=True)
            values = v_buf[slot, :, g * W : (g + 1) * W]
            o = jnp.dot(p.astype(BF), values, preferred_element_type=F32)
            rows = pl.ds(g * HALF + slot, PER, SLOTS)
            out_ref[rows, :] = o / total
            lse_ref[rows, :] = jnp.broadcast_to(top + jnp.log2(total), (PER, W))


def suffix(lengths, q, keys, values):
    shape = jax.ShapeDtypeStruct((ROWS, W), F32)
    return pl.pallas_call(
        suffix_kernel,
        in_specs=[pl.BlockSpec(memory_space=pltpu.SMEM), VMEM, HBM, HBM],
        out_specs=(VMEM, VMEM),
        out_shape=(shape, shape),
        scratch_shapes=[
            pltpu.VMEM(keys.shape, BF),
            pltpu.VMEM(keys.shape, BF),
            pltpu.SemaphoreType.DMA((2 * SLOTS,)),
        ],
        compiler_params=params(58),
        cost_estimate=pl.CostEstimate(
            flops=4 * HEADS * W * keys.shape[0] * keys.shape[1],
            bytes_accessed=8 * MIB,
            transcendentals=SLOTS * HEADS * keys.shape[1],
        ),
        name="suffix_attention",
    )(lengths, q, keys, values)


def pieces(lse):
    high = lse.astype(BF).astype(F32)
    middle = (lse - high).astype(BF).astype(F32)
    return high, middle, (lse - high) - middle


def prompt_kernel(count, *refs):
    q_refs, (k0, k1, v0, v1) = refs[:count], refs[count : count + 4]
    out_refs, v_buf = refs[count + 4 : 2 * count + 4], refs[2 * count + 4]
    span = k0.shape[0]
    for half, v in enumerate((v0, v1)):
        for g in range(KV):
            v_buf[g, half * span : (half + 1) * span, :W] = v[:, g * W : (g + 1) * W]
    v_buf[:, :, W:] = jnp.ones((KV, 2 * span, W), BF)

    total_rows = count * Z * HALF
    lane = lax.broadcasted_iota(jnp.int32, (total_rows, W), 1)
    marks = []
    for g in range(KV):
        q = [ref[:, g * HALF : (g + 1) * HALF, :].reshape(Z * HALF, W) for ref in q_refs]
        q = jnp.concatenate(q, axis=0) if count > 1 else q[0]
        top = jnp.full((total_rows, 1), -1e30, F32)
        o = jnp.zeros((total_rows, 2 * W), F32)
        for at in range(0, 2 * span, CHUNK):
            keys = (k0, k1)[at // span][at % span : at % span + CHUNK, g * W : (g + 1) * W]
            s = lax.dot_general(q, keys, NT, preferred_element_type=F32)
            new = jnp.maximum(top, jnp.max(s, axis=1, keepdims=True) * TO_LOG2)
            p = jnp.exp2(s * TO_LOG2 - new).astype(BF)
            o = o * jnp.exp2(top - new) + jnp.dot(p, v_buf[g, at : at + CHUNK, :], preferred_element_type=F32)
            top = new
        total = o[:, W:]
        mean = (o[:, :W] / total).astype(BF).reshape(count, Z, HALF, W)
        for i, out_ref in enumerate(out_refs):
            out_ref[:, g * HALF : (g + 1) * HALF, :] = mean[i]
        high, middle, low = pieces(top + jnp.log2(total))
        mark = jnp.where(lane == 0, high, jnp.where(lane == 1, middle, jnp.where(lane == 2, low, 0.0)))
        marks.append(mark.astype(BF).reshape(count, Z, HALF, W))
    pick = (
        lax.broadcasted_iota(jnp.int32, (16, W), 0) == lax.broadcasted_iota(jnp.int32, (16, W), 1)
    ).astype(BF)
    nothing = jnp.zeros((W - ROWS, W), BF)
    for i, out_ref in enumerate(out_refs):
        for z in range(Z):
            column = jnp.concatenate([marks[0][i, z], marks[1][i, z], nothing], axis=0)
            row = lax.dot_general(pick, column, NT, preferred_element_type=F32)
            out_ref[z, ROWS:PACKED, :] = row.astype(BF)


def prompt(qs, ks, vs, name):
    count, span = len(qs), 2 * ks[0].shape[0]
    out = jax.ShapeDtypeStruct((Z, PACKED, W), BF)
    return pl.pallas_call(
        functools.partial(prompt_kernel, count),
        out_shape=[out] * count,
        scratch_shapes=[pltpu.VMEM((KV, span, 2 * W), BF)],
        compiler_params=params(32),
        cost_estimate=pl.CostEstimate(
            flops=4 * count * Z * ROWS * span * W,
            bytes_accessed=5 * MIB,
            transcendentals=count * Z * ROWS * span,
        ),
        name=name,
    )(*qs, *ks, *vs)


def lse_rows(ref):
    marks = ref[:, ROWS:PACKED, :].astype(F32)
    return marks[:, 0, :] + marks[:, 1, :] + marks[:, 2, :]


def turned(rows):
    return jnp.concatenate([rows, jnp.zeros((W - rows.shape[0], W), F32)], axis=0).T[:ROWS]


def merge_kernel(id_ref, p0, p1, p2, p3, out_ref):
    parts = (p0, p1, p2, p3)
    lses = [lse_rows(p) for p in parts]
    top = functools.reduce(jnp.maximum, lses)
    shares = [jnp.exp2(lse - top) for lse in lses]
    total = functools.reduce(jnp.add, shares)
    columns = turned(jnp.concatenate([share / total for share in shares], axis=0))
    new = pieces(top + jnp.log2(total))
    row = lax.broadcasted_iota(jnp.int32, (16, W), 0)
    lane = lax.broadcasted_iota(jnp.int32, (16, W), 1)
    ids = jnp.zeros((16, W), jnp.int32)
    for slot in range(SLOTS):
        ids = jnp.where((row == 3) & (lane == ROWS + slot), id_ref[slot], ids)
    ids = ids.astype(F32)
    for z in range(Z):
        terms = [
            p[z, :ROWS, :].astype(F32) * columns[:, i * Z + z : i * Z + z + 1] for i, p in enumerate(parts)
        ]
        out_ref[z, :ROWS, :] = ((terms[0] + terms[1]) + (terms[2] + terms[3])).astype(BF)
        tile = ids
        for i, piece in enumerate(new):
            tile = jnp.where(row == i, piece[z : z + 1, :], tile)
        out_ref[z, ROWS:PACKED, :] = tile.astype(BF)


def merge(ids, parts):
    return pl.pallas_call(
        merge_kernel,
        in_specs=[pl.BlockSpec(memory_space=pltpu.SMEM)] + [VMEM] * X,
        out_specs=VMEM,
        out_shape=jax.ShapeDtypeStruct((Z, PACKED, W), BF),
        compiler_params=params(8),
        name="merge_along_x",
    )(ids, *parts)


def combine_kernel(part_ref, suffix_ref, suffix_lse_ref, out_ref):
    lse = turned(lse_rows(part_ref))[:, :Z]
    own = suffix_lse_ref[...]
    top = jnp.maximum(jnp.max(lse, axis=1, keepdims=True), jnp.max(own, axis=1, keepdims=True))
    share = jnp.exp2(lse - top)
    own_share = jnp.exp2(own - top)
    total = jnp.sum(share, axis=1, keepdims=True) + own_share
    sums = [suffix_ref[...] * own_share, jnp.zeros((ROWS, W), F32)]
    for z in range(Z):
        sums[z % 2] += part_ref[z, :ROWS, :].astype(F32) * share[:, z : z + 1]
    attention = ((sums[0] + sums[1]) / total).astype(BF)
    for z in range(Z):
        out_ref[z] = attention


def combine(parts, suffix_out, suffix_lse):
    return pl.pallas_call(
        combine_kernel,
        out_shape=jax.ShapeDtypeStruct((Z, ROWS, W), BF),
        compiler_params=params(8),
        name="combine_along_z",
    )(parts, suffix_out, suffix_lse)


def tick_kernel(a_ref, b_ref, c_ref, d_ref):
    c_ref[...] = a_ref[...]
    d_ref[...] = b_ref[...]


def tick(a, b):
    return pl.pallas_call(
        tick_kernel,
        out_shape=tuple(jax.ShapeDtypeStruct(x.shape, x.dtype) for x in (a, b)),
        compiler_params=params(8),
        cost_estimate=pl.CostEstimate(flops=0, bytes_accessed=4 * MIB, transcendentals=0),
        name="bring_suffix",
    )(a, b)


def project_kernel(at_ref, a_ref, b_ref, id_ref, *refs):
    w_refs, (out_ref, cat_ref) = refs[:X], refs[X:]
    group = 4
    size = group * ROWS
    near = lax.broadcasted_iota(jnp.int32, (size, size), 0)
    far = lax.broadcasted_iota(jnp.int32, (size, size), 1)
    tall = group * SLOTS
    wanted = ((near % tall) // SLOTS) * ROWS + (near // tall) * SLOTS + near % SLOTS
    sort = (wanted == far).astype(BF)
    for i in range(CORES * Z // group):
        half, first = divmod(i * group, Z)
        rows = (a_ref, b_ref)[half][first : first + group].reshape(size, W)
        rows = jnp.dot(sort, rows, preferred_element_type=F32).astype(BF)
        for h in range(HEADS):
            cat_ref[i * tall : (i + 1) * tall, h * W : (h + 1) * W] = rows[h * tall : (h + 1) * tall, :]
    count = CORES * Z * SLOTS
    for block, w_ref in enumerate(w_refs):
        projected = jnp.dot(cat_ref[...], w_ref[...], preferred_element_type=F32).astype(BF)
        to = lax.rem(at_ref[0] + block, X) * Y
        for y in range(Y):
            out_ref[to + y, :count, :] = projected
            out_ref[to + y, count:, :] = id_ref[...]


def project(at, own, others, ids, weights):
    count = CORES * Z * SLOTS
    return pl.pallas_call(
        project_kernel,
        in_specs=[pl.BlockSpec(memory_space=pltpu.SMEM)] + [VMEM] * (3 + len(weights)),
        out_specs=VMEM,
        out_shape=jax.ShapeDtypeStruct((X * Y, count + 16, W), BF),
        scratch_shapes=[pltpu.VMEM((count, HEADS * W), BF)],
        compiler_params=params(16),
        name="project",
    )(at, own, others, ids, *weights)


def finish_kernel(at_ref, part_ref, out_ref):
    count = CORES * Z * SLOTS
    ids = lax.broadcasted_iota(jnp.int32, (out_ref.shape[0], W), 0) + at_ref[1] * out_ref.shape[0]
    result = jnp.zeros(out_ref.shape, F32)
    for block in range(X):
        part = [part_ref[block * Y + y, :count, :].astype(F32) for y in range(Y)]
        rows = ((part[0] + part[1]) + (part[2] + part[3])).astype(BF)
        owner = part_ref[block * Y, count:, :].astype(F32)[:1, :].astype(jnp.int32)
        select = (ids == owner).astype(BF)[:, :count]
        result += jnp.dot(select, rows, preferred_element_type=F32)
    out_ref[...] = result.astype(BF)


def finish(at, parts):
    return pl.pallas_call(
        finish_kernel,
        in_specs=[pl.BlockSpec(memory_space=pltpu.SMEM), VMEM],
        out_specs=VMEM,
        out_shape=jax.ShapeDtypeStruct((X * CORES * Z * SLOTS // Y, W), BF),
        compiler_params=params(8),
        name="finish",
    )(at, parts)


def place(x, z, c):
    return (x * Z + z) * CORES + c


OTHER_CORE = [(i, i ^ 1) for i in range(X * Z * CORES)]
ALONG_Z = [[place(x, z, c) for z in range(Z)] for x in range(X) for c in range(CORES)]
X_Y = [
    [place(x, z, c) * Y + y for x in range(X) for y in range(Y)] for z in range(Z) for c in range(CORES)
]


def other(a):
    return lax.ppermute(a, "seq", OTHER_CORE)


def shift(a, by):
    pairs = [
        (place(x, z, c), place((x + by) % X, z, c)) for x in range(X) for z in range(Z) for c in range(CORES)
    ]
    return lax.ppermute(a, "seq", pairs)


def exchange(a, groups, axes="seq"):
    return lax.all_to_all(a, axes, 0, 0, axis_index_groups=groups, tiled=True)


def on_device(queries, prompt_keys, prompt_values, keys, values, lengths, slot_sample, out_weight):
    after = lax.optimization_barrier
    at = jnp.stack([lax.axis_index("seq") // (Z * CORES), lax.axis_index("head")]).astype(jnp.int32)
    block, rows = spread(queries)
    block, prompt_keys, prompt_values, out_weight = after((block, prompt_keys, prompt_values, out_weight))
    own = exchange(block, ALONG_Z)
    ks, vs = (prompt_keys, other(prompt_keys)), (prompt_values, other(prompt_values))
    weights = {0: out_weight, 1: shift(out_weight, -1)}
    away = [shift(own, -d) for d in range(1, X)]
    (own_part,) = prompt([own], ks, vs, "prompt_own")
    own_part, weights[1], *away = after((own_part, weights[1], *away))
    away_parts = prompt(away, ks, vs, "prompt_away")
    *away_parts, rows = after((*away_parts, rows))
    away_parts = [shift(a, d) for d, a in zip(range(1, X), away_parts)]
    suffix_out, suffix_lse = suffix(lengths, rows, keys, values)
    suffix_out, suffix_lse, *away_parts = after((suffix_out, suffix_lse, *away_parts))
    merged = merge(slot_sample, [own_part, *away_parts])
    merged, suffix_out, suffix_lse = after((merged, suffix_out, suffix_lse))
    parts = exchange(merged, ALONG_Z)
    suffix_out, suffix_lse, weight, next_weight = after(
        (*tick(suffix_out, suffix_lse), out_weight, weights[1])
    )
    weights[2], weights[3] = shift(next_weight, -1), shift(weight, 1)
    attention = exchange(combine(parts, suffix_out, suffix_lse), ALONG_Z)
    owner = parts[:, ROWS + 3, ROWS : ROWS + SLOTS].reshape(1, Z * SLOTS)
    owner = jnp.concatenate([owner, other(jnp.broadcast_to(owner, (8, Z * SLOTS)))[:1]], axis=1)
    owner = jnp.pad(owner, ((0, 15), (0, W - CORES * Z * SLOTS)))
    placed = project(at, attention, other(attention), owner, [weights[d] for d in range(X)])
    return finish(at, exchange(placed, X_Y, ("seq", "head")))


def solution(mesh):
    return jax.shard_map(
        on_device,
        mesh=mesh,
        in_specs=(
            P("seq", "head"),
            P("seq", "head"),
            P("seq", "head"),
            P("seq", None, "head"),
            P("seq", None, "head"),
            P("seq"),
            P("seq"),
            P("head", "seq"),
        ),
        out_specs=P("head", "seq"),
        check_vma=False,
    )
```

```python
import functools

import jax
import jax.numpy as jnp
import numpy as np
from jax import lax
from jax.experimental import pallas as pl
from jax.experimental.pallas import tpu as pltpu
from jax.sharding import PartitionSpec as P

HEADS = 16
KV = 2
PER = 8
W = 128
SLOTS = 4
X, Z, CORES, Y = 4, 8, 2, 4
ROWS = HEADS * SLOTS
HALF = ROWS // KV
PACKED = ROWS + 16
CHUNK = 512
MIB = 1 << 20
BF, F32 = jnp.bfloat16, jnp.float32
TO_LOG2 = float(np.log2(np.e) * W**-0.5)
NT = (((1,), (1,)), ((), ()))


VMEM = pl.BlockSpec(memory_space=pltpu.VMEM)
HBM = pl.BlockSpec(memory_space=pltpu.HBM)


def params(limit):
    return pltpu.CompilerParams(vmem_limit_bytes=limit * MIB)


def spread_kernel(q_ref, out_ref, rows_ref):
    q = q_ref[...].astype(F32)
    rows = jnp.concatenate([q[:, h * W : (h + 1) * W] for h in range(HEADS)], axis=0)
    rows_ref[...] = rows
    block = rows.astype(BF)
    for chip in range(Z):
        out_ref[chip] = block


def spread(queries):
    return pl.pallas_call(
        spread_kernel,
        out_shape=(jax.ShapeDtypeStruct((Z, ROWS, W), BF), jax.ShapeDtypeStruct((ROWS, W), F32)),
        compiler_params=params(8),
        name="spread_queries",
    )(queries)


def suffix_kernel(length_ref, q_ref, k_ref, v_ref, out_ref, lse_ref, k_buf, v_buf, sems):
    span = k_ref.shape[1]
    copies = []
    for slot in range(SLOTS):
        for i, (ref, buf) in enumerate(((k_ref, k_buf), (v_ref, v_buf))):
            copies.append(pltpu.make_async_copy(ref.at[slot], buf.at[slot], sems.at[2 * slot + i]))
            copies[-1].start()
    at = lax.broadcasted_iota(jnp.int32, (PER, span), 1)
    for slot in range(SLOTS):
        copies[2 * slot].wait()
        scores = []
        for g in range(KV):
            keys = k_buf[slot, :, g * W : (g + 1) * W]
            s = lax.dot_general(q_ref[pl.ds(g * HALF + slot, PER, SLOTS), :].astype(BF), keys, NT, preferred_element_type=F32)
            scores.append(jnp.where(at < length_ref[slot], s * TO_LOG2, -1e30))
        copies[2 * slot + 1].wait()
        for g in range(KV):
            top = jnp.max(scores[g], axis=1, keepdims=True)
            p = jnp.exp2(scores[g] - top)
            total = jnp.sum(p, axis=1, keepdims=True)
            values = v_buf[slot, :, g * W : (g + 1) * W]
            o = jnp.dot(p.astype(BF), values, preferred_element_type=F32)
            rows = pl.ds(g * HALF + slot, PER, SLOTS)
            out_ref[rows, :] = o / total
            lse_ref[rows, :] = jnp.broadcast_to(top + jnp.log2(total), (PER, W))


def suffix(lengths, q, keys, values):
    shape = jax.ShapeDtypeStruct((ROWS, W), F32)
    return pl.pallas_call(
        suffix_kernel,
        in_specs=[pl.BlockSpec(memory_space=pltpu.SMEM), VMEM, HBM, HBM],
        out_specs=(VMEM, VMEM),
        out_shape=(shape, shape),
        scratch_shapes=[
            pltpu.VMEM(keys.shape, BF),
            pltpu.VMEM(keys.shape, BF),
            pltpu.SemaphoreType.DMA((2 * SLOTS,)),
        ],
        compiler_params=params(58),
        cost_estimate=pl.CostEstimate(
            flops=4 * HEADS * W * keys.shape[0] * keys.shape[1],
            bytes_accessed=8 * MIB,
            transcendentals=SLOTS * HEADS * keys.shape[1],
        ),
        name="suffix_attention",
    )(lengths, q, keys, values)


def pieces(lse):
    high = lse.astype(BF).astype(F32)
    middle = (lse - high).astype(BF).astype(F32)
    return high, middle, (lse - high) - middle


def prompt_kernel(count, *refs):
    q_refs, (k0, k1, v0, v1) = refs[:count], refs[count : count + 4]
    out_refs, v_buf = refs[count + 4 : 2 * count + 4], refs[2 * count + 4]
    span = k0.shape[0]
    for half, v in enumerate((v0, v1)):
        for g in range(KV):
            v_buf[g, half * span : (half + 1) * span, :W] = v[:, g * W : (g + 1) * W]
    v_buf[:, :, W:] = jnp.ones((KV, 2 * span, W), BF)

    total_rows = count * Z * HALF
    lane = lax.broadcasted_iota(jnp.int32, (total_rows, W), 1)
    marks = []
    for g in range(KV):
        q = [ref[:, g * HALF : (g + 1) * HALF, :].reshape(Z * HALF, W) for ref in q_refs]
        q = jnp.concatenate(q, axis=0) if count > 1 else q[0]
        top = jnp.full((total_rows, 1), -1e30, F32)
        o = jnp.zeros((total_rows, 2 * W), F32)
        for at in range(0, 2 * span, CHUNK):
            keys = (k0, k1)[at // span][at % span : at % span + CHUNK, g * W : (g + 1) * W]
            s = lax.dot_general(q, keys, NT, preferred_element_type=F32)
            new = jnp.maximum(top, jnp.max(s, axis=1, keepdims=True) * TO_LOG2)
            p = jnp.exp2(s * TO_LOG2 - new).astype(BF)
            o = o * jnp.exp2(top - new) + jnp.dot(p, v_buf[g, at : at + CHUNK, :], preferred_element_type=F32)
            top = new
        total = o[:, W:]
        mean = (o[:, :W] / total).astype(BF).reshape(count, Z, HALF, W)
        for i, out_ref in enumerate(out_refs):
            out_ref[:, g * HALF : (g + 1) * HALF, :] = mean[i]
        high, middle, low = pieces(top + jnp.log2(total))
        mark = jnp.where(lane == 0, high, jnp.where(lane == 1, middle, jnp.where(lane == 2, low, 0.0)))
        marks.append(mark.astype(BF).reshape(count, Z, HALF, W))
    pick = (
        lax.broadcasted_iota(jnp.int32, (16, W), 0) == lax.broadcasted_iota(jnp.int32, (16, W), 1)
    ).astype(BF)
    nothing = jnp.zeros((W - ROWS, W), BF)
    for i, out_ref in enumerate(out_refs):
        for z in range(Z):
            column = jnp.concatenate([marks[0][i, z], marks[1][i, z], nothing], axis=0)
            row = lax.dot_general(pick, column, NT, preferred_element_type=F32)
            out_ref[z, ROWS:PACKED, :] = row.astype(BF)


def prompt(qs, ks, vs, name):
    count, span = len(qs), 2 * ks[0].shape[0]
    out = jax.ShapeDtypeStruct((Z, PACKED, W), BF)
    return pl.pallas_call(
        functools.partial(prompt_kernel, count),
        out_shape=[out] * count,
        scratch_shapes=[pltpu.VMEM((KV, span, 2 * W), BF)],
        compiler_params=params(32),
        cost_estimate=pl.CostEstimate(
            flops=4 * count * Z * ROWS * span * W,
            bytes_accessed=5 * MIB,
            transcendentals=count * Z * ROWS * span,
        ),
        name=name,
    )(*qs, *ks, *vs)


def lse_rows(ref):
    marks = ref[:, ROWS:PACKED, :].astype(F32)
    return marks[:, 0, :] + marks[:, 1, :] + marks[:, 2, :]


def turned(rows):
    return jnp.concatenate([rows, jnp.zeros((W - rows.shape[0], W), F32)], axis=0).T[:ROWS]


def merge_kernel(id_ref, p0, p1, p2, p3, out_ref):
    parts = (p0, p1, p2, p3)
    lses = [lse_rows(p) for p in parts]
    top = functools.reduce(jnp.maximum, lses)
    shares = [jnp.exp2(lse - top) for lse in lses]
    total = functools.reduce(jnp.add, shares)
    columns = turned(jnp.concatenate([share / total for share in shares], axis=0))
    new = pieces(top + jnp.log2(total))
    row = lax.broadcasted_iota(jnp.int32, (16, W), 0)
    lane = lax.broadcasted_iota(jnp.int32, (16, W), 1)
    ids = jnp.zeros((16, W), jnp.int32)
    for slot in range(SLOTS):
        ids = jnp.where((row == 3) & (lane == ROWS + slot), id_ref[slot], ids)
    ids = ids.astype(F32)
    for z in range(Z):
        terms = [
            p[z, :ROWS, :].astype(F32) * columns[:, i * Z + z : i * Z + z + 1] for i, p in enumerate(parts)
        ]
        out_ref[z, :ROWS, :] = ((terms[0] + terms[1]) + (terms[2] + terms[3])).astype(BF)
        tile = ids
        for i, piece in enumerate(new):
            tile = jnp.where(row == i, piece[z : z + 1, :], tile)
        out_ref[z, ROWS:PACKED, :] = tile.astype(BF)


def merge(ids, parts):
    return pl.pallas_call(
        merge_kernel,
        in_specs=[pl.BlockSpec(memory_space=pltpu.SMEM)] + [VMEM] * X,
        out_specs=VMEM,
        out_shape=jax.ShapeDtypeStruct((Z, PACKED, W), BF),
        compiler_params=params(8),
        name="merge_along_x",
    )(ids, *parts)


def combine_kernel(part_ref, suffix_ref, suffix_lse_ref, out_ref):
    lse = turned(lse_rows(part_ref))[:, :Z]
    own = suffix_lse_ref[...]
    top = jnp.maximum(jnp.max(lse, axis=1, keepdims=True), jnp.max(own, axis=1, keepdims=True))
    share = jnp.exp2(lse - top)
    own_share = jnp.exp2(own - top)
    total = jnp.sum(share, axis=1, keepdims=True) + own_share
    sums = [suffix_ref[...] * own_share, jnp.zeros((ROWS, W), F32)]
    for z in range(Z):
        sums[z % 2] += part_ref[z, :ROWS, :].astype(F32) * share[:, z : z + 1]
    attention = ((sums[0] + sums[1]) / total).astype(BF)
    for z in range(Z):
        out_ref[z] = attention


def combine(parts, suffix_out, suffix_lse):
    return pl.pallas_call(
        combine_kernel,
        out_shape=jax.ShapeDtypeStruct((Z, ROWS, W), BF),
        compiler_params=params(8),
        name="combine_along_z",
    )(parts, suffix_out, suffix_lse)


def tick_kernel(a_ref, b_ref, c_ref, d_ref):
    c_ref[...] = a_ref[...]
    d_ref[...] = b_ref[...]


def tick(a, b):
    return pl.pallas_call(
        tick_kernel,
        out_shape=tuple(jax.ShapeDtypeStruct(x.shape, x.dtype) for x in (a, b)),
        compiler_params=params(8),
        cost_estimate=pl.CostEstimate(flops=0, bytes_accessed=4 * MIB, transcendentals=0),
        name="bring_suffix",
    )(a, b)


def project_kernel(at_ref, a_ref, b_ref, id_ref, *refs):
    w_refs, (out_ref, cat_ref) = refs[:X], refs[X:]
    group = 4
    size = group * ROWS
    near = lax.broadcasted_iota(jnp.int32, (size, size), 0)
    far = lax.broadcasted_iota(jnp.int32, (size, size), 1)
    tall = group * SLOTS
    wanted = ((near % tall) // SLOTS) * ROWS + (near // tall) * SLOTS + near % SLOTS
    sort = (wanted == far).astype(BF)
    for i in range(CORES * Z // group):
        half, first = divmod(i * group, Z)
        rows = (a_ref, b_ref)[half][first : first + group].reshape(size, W)
        rows = jnp.dot(sort, rows, preferred_element_type=F32).astype(BF)
        for h in range(HEADS):
            cat_ref[i * tall : (i + 1) * tall, h * W : (h + 1) * W] = rows[h * tall : (h + 1) * tall, :]
    count = CORES * Z * SLOTS
    for block, w_ref in enumerate(w_refs):
        projected = jnp.dot(cat_ref[...], w_ref[...], preferred_element_type=F32).astype(BF)
        to = lax.rem(at_ref[0] + block, X) * Y
        for y in range(Y):
            out_ref[to + y, :count, :] = projected
            out_ref[to + y, count:, :] = id_ref[...]


def project(at, own, others, ids, weights):
    count = CORES * Z * SLOTS
    return pl.pallas_call(
        project_kernel,
        in_specs=[pl.BlockSpec(memory_space=pltpu.SMEM)] + [VMEM] * (3 + len(weights)),
        out_specs=VMEM,
        out_shape=jax.ShapeDtypeStruct((X * Y, count + 16, W), BF),
        scratch_shapes=[pltpu.VMEM((count, HEADS * W), BF)],
        compiler_params=params(16),
        name="project",
    )(at, own, others, ids, *weights)


def finish_kernel(at_ref, part_ref, out_ref):
    count = CORES * Z * SLOTS
    ids = lax.broadcasted_iota(jnp.int32, (out_ref.shape[0], W), 0) + at_ref[1] * out_ref.shape[0]
    result = jnp.zeros(out_ref.shape, F32)
    for block in range(X):
        part = [part_ref[block * Y + y, :count, :].astype(F32) for y in range(Y)]
        rows = ((part[0] + part[1]) + (part[2] + part[3])).astype(BF)
        owner = part_ref[block * Y, count:, :].astype(F32)[:1, :].astype(jnp.int32)
        select = (ids == owner).astype(BF)[:, :count]
        result += jnp.dot(select, rows, preferred_element_type=F32)
    out_ref[...] = result.astype(BF)


def finish(at, parts):
    return pl.pallas_call(
        finish_kernel,
        in_specs=[pl.BlockSpec(memory_space=pltpu.SMEM), VMEM],
        out_specs=VMEM,
        out_shape=jax.ShapeDtypeStruct((X * CORES * Z * SLOTS // Y, W), BF),
        compiler_params=params(8),
        name="finish",
    )(at, parts)


def place(x, z, c):
    return (x * Z + z) * CORES + c


OTHER_CORE = [(i, i ^ 1) for i in range(X * Z * CORES)]
ALONG_Z = [[place(x, z, c) for z in range(Z)] for x in range(X) for c in range(CORES)]
X_Y = [
    [place(x, z, c) * Y + y for x in range(X) for y in range(Y)] for z in range(Z) for c in range(CORES)
]


def other(a):
    return lax.ppermute(a, "seq", OTHER_CORE)


def shift(a, by):
    pairs = [
        (place(x, z, c), place((x + by) % X, z, c)) for x in range(X) for z in range(Z) for c in range(CORES)
    ]
    return lax.ppermute(a, "seq", pairs)


def exchange(a, groups, axes="seq"):
    return lax.all_to_all(a, axes, 0, 0, axis_index_groups=groups, tiled=True)


def on_device(queries, prompt_keys, prompt_values, keys, values, lengths, slot_sample, out_weight):
    after = lax.optimization_barrier
    at = jnp.stack([lax.axis_index("seq") // (Z * CORES), lax.axis_index("head")]).astype(jnp.int32)
    block, rows = spread(queries)
    block, prompt_keys, prompt_values, out_weight = after((block, prompt_keys, prompt_values, out_weight))
    own = exchange(block, ALONG_Z)
    ks, vs = (prompt_keys, other(prompt_keys)), (prompt_values, other(prompt_values))
    weights = {0: out_weight, 1: shift(out_weight, -1)}
    far_first = (2, 1, 3)
    away = [shift(own, -d) for d in far_first]
    (own_part,) = prompt([own], ks, vs, "prompt_own")
    own_part, weights[1], *away = after((own_part, weights[1], *away))
    away_parts = prompt(away, ks, vs, "prompt_away")
    *away_parts, rows = after((*away_parts, rows))
    away_parts = [shift(a, d) for d, a in zip(far_first, away_parts)]
    suffix_out, suffix_lse = suffix(lengths, rows, keys, values)
    suffix_out, suffix_lse, *away_parts = after((suffix_out, suffix_lse, *away_parts))
    merged = merge(slot_sample, [own_part, *away_parts])
    merged, suffix_out, suffix_lse = after((merged, suffix_out, suffix_lse))
    parts = exchange(merged, ALONG_Z)
    suffix_out, suffix_lse, weight, next_weight = after(
        (*tick(suffix_out, suffix_lse), out_weight, weights[1])
    )
    weights[2], weights[3] = shift(next_weight, -1), shift(weight, 1)
    attention = exchange(combine(parts, suffix_out, suffix_lse), ALONG_Z)
    owner = parts[:, ROWS + 3, ROWS : ROWS + SLOTS].reshape(1, Z * SLOTS)
    owner = jnp.concatenate([owner, other(jnp.broadcast_to(owner, (8, Z * SLOTS)))[:1]], axis=1)
    owner = jnp.pad(owner, ((0, 15), (0, W - CORES * Z * SLOTS)))
    placed = project(at, attention, other(attention), owner, [weights[d] for d in range(X)])
    return finish(at, exchange(placed, X_Y, ("seq", "head")))


def solution(mesh):
    return jax.shard_map(
        on_device,
        mesh=mesh,
        in_specs=(
            P("seq", "head"),
            P("seq", "head"),
            P("seq", "head"),
            P("seq", None, "head"),
            P("seq", None, "head"),
            P("seq"),
            P("seq"),
            P("head", "seq"),
        ),
        out_specs=P("head", "seq"),
        check_vma=False,
    )
```
